32 devices in a mesh: group: 2 (over x), tensor: 16 (over z, y, core).
Axes of the slice: x: 2, y: 2, z: 4, core: 2. Of those that a mesh axis runs over, the one named last changes fastest.
Arguments:
- tokens_in: bfloat16 [64, 5120], P('group', 'tensor'), parts along dimension 0, may hold values from -20 to 20
- norm_gain: float32 [5120], P('tensor'), may hold values from 0.1 to 1.9
- w_qkv: bfloat16 [5120, 7168], P('tensor'), may hold values from -0.078125 to 0.078125
- w_out: bfloat16 [5120, 5120], P(None, 'tensor'), may hold values from -0.078125 to 0.078125
- cache_keys: bfloat16 [64, 96, 1024], P(('group', 'tensor')), parts along dimension 0, may hold values from -240 to 240
- cache_values: bfloat16 [64, 96, 1024], P(('group', 'tensor')), parts along dimension 0, may hold values from -6 to 6
- kv_lengths: int32 [64], P(('group', 'tensor')), parts along dimension 0, may hold values from 1 to 96
- w_cond: bfloat16 [5120, 1536], P('tensor'), may hold values from -0.078125 to 0.078125
- w_embed: bfloat16 [16, 5120], P(None, 'tensor'), may hold values from -1.5 to 1.5
- placement: int32 [64, 1], P('group'), parts along dimension 0, may hold values from 0 to 15; in each aligned block of 32 rows (0 to 31, 32 to 63, ...) at most 8 rows name the same one
- noise: float32 [2, 256, 16], P(None, ('group', 'tensor')), parts along dimension 1, may hold values from -5 to 5
- w_latent: bfloat16 [16, 1536], replicated, may hold values from -1.5 to 1.5
- w_up: bfloat16 [1536, 1536], replicated, may hold values from -0.15625 to 0.15625
- w_down: bfloat16 [1536, 1536], replicated, may hold values from -0.15625 to 0.15625
- w_vel: bfloat16 [1536, 16], replicated, may hold values from -0.15625 to 0.15625
- head_gain: float32 [1536], replicated, may hold values from 0.1 to 1.9
Outputs:
- latents: float32 [2, 64, 16], P(None, ('group', 'tensor')), parts along dimension 1
- hidden: bfloat16 [64, 5120], P('group', 'tensor'), parts along dimension 0
The draws below stay inside these ranges and needn't reach their ends.
There are 2 independent parts, one for each index of `group`. The reference program is written for one: setup_inputs(seed, part) draws one part's arguments, and reference() takes and returns one part's arrays. A program takes and returns all parts, laid end to end along the dimension named above; an argument that names none is the same for every part. Nothing has to cross between parts.
Inputs may be any that keep to these rules, and one draw needn't show every extreme that they name: `placement`: at most 8 requests share a head device, and one head device has exactly 8.
All inputs are finite; a program needn't handle non-finite values.
Results may differ from the reference program's by a relative error of at most 0.025.
Values may be sent and summed in bfloat16 or wider, within the bound.
A program may use at most 64 MiB of HBM per device.

```python
import math
import jax
import jax.numpy as jnp
import numpy as np
from jax import lax

D = 5120
HEADS = 40
KVH = 8
HD = 128
HW = 1536
LAT = 16
STEPS = 8
CACHE = 96
REQ = 32
QKVW = 7168
HCAP = 8
SLOTS = 128
N_TENSOR = 16


def draw_tokens_in(key, part):
    key = jax.random.fold_in(key, 13)
    position = jnp.arange(D, dtype=jnp.float32)[None, :] / (D - 1)
    values = jnp.clip(jax.random.normal(key, (REQ, D), jnp.float32), -6.0, 6.0) * (0.4 * jnp.exp(math.log(8.0) * position))
    return values.astype(jnp.bfloat16)


def draw_cache_keys(key, part):
    key = jax.random.fold_in(key, 11)
    values = jnp.clip(jax.random.normal(key, (REQ, CACHE, KVH * HD), jnp.float32), -6.0, 6.0)
    return values.astype(jnp.bfloat16)


def draw_kv_lengths(key, part):
    key = jax.random.fold_in(key, 12)
    lengths = jax.random.randint(key, (REQ,), 1, CACHE + 1)
    chosen = jax.random.randint(jax.random.fold_in(key, 1), (), 0, REQ)
    return jnp.where(jnp.arange(REQ) == chosen, CACHE, lengths).astype(jnp.int32)


def levels(stream_key, dims, cuts, low, top_value):
    level, own = 1.0, jax.random.fold_in(stream_key, 6)
    for dim, blocks in cuts:
        heights = jnp.exp(jax.random.uniform(jax.random.fold_in(own, dim), (blocks,), jnp.float32, low / len(cuts), top_value / len(cuts)))
        level = level * jnp.repeat(heights, dims[dim] // blocks).reshape([-1 if axis == dim else 1 for axis in range(len(dims))])
    return level


def deal_out(rng, own, number, rows, count, top, bound, lean):
    sequence = jax.random.permutation(rng, count)
    heavy_load, ordinary = load_shares(count, rows * top, bound, lean, True), load_shares(count, rows * top, bound, lean, False)
    places = jnp.arange(count)

    def named(sizes, turn):
        used = int((sizes > 0).sum())
        fixed = max(1, used // 4)
        moved = fixed + (places - fixed + turn * (used - fixed)) % max(1, count - fixed)
        return jnp.zeros((count,), jnp.int32).at[sequence[jnp.where(places < fixed, places, moved)]].set(jnp.asarray(sizes, jnp.int32))

    sizes = jnp.where(number % 4 == 0, named(heavy_load, number // 4), named(ordinary, number - number // 4 - 1))
    mixed = jax.random.permutation(jax.random.fold_in(own, 3), count)
    giver, taker = mixed[0:count // 2 * 2:2], mixed[1:count // 2 * 2:2]
    margin = jnp.minimum(sizes[giver] - 1, bound - sizes[taker]) // 2
    margin = jnp.where((giver == sequence[0]) | (taker == sequence[0]) | (sizes[taker] == 0), 0, jnp.maximum(margin, 0))
    moved = jax.random.randint(jax.random.fold_in(own, 4), (count // 2,), 0, 1 << 20) % (margin + 1)
    sizes = sizes.at[giver].add(-moved).at[taker].add(moved)
    members = jnp.searchsorted(jnp.cumsum(sizes), jnp.arange(rows * top), side="right").astype(jnp.int32)
    grid = members.reshape(top, rows).T
    grid = grid[jax.random.permutation(jax.random.fold_in(own, 1), rows)]
    turn = jax.random.randint(jax.random.fold_in(own, 2), (rows, 1), 0, top)
    return jnp.take_along_axis(grid, (jnp.arange(top)[None, :] + turn) % top, axis=1)


def load_shares(count, total, most, skew, full):
    portions = [(1 << 20) // math.isqrt(grade ** skew) + 1 for grade in range(1, count + 1)]
    largest = most if full else min(most, max(-(-total // count), total * portions[0] // sum(portions)))
    least = 1 if total - largest >= count - 1 else 0
    holding, surplus = [largest] + [least] * (count - 1), total - largest - least * (count - 1)
    while surplus > 0:
        movable = [i for i in range(1, count) if holding[i] < largest] or [i for i in range(1, count) if holding[i] < most]
        whole, budget = sum([portions[i] for i in movable]), surplus
        for i in movable:
            addition = min(most - holding[i], max(1, budget * portions[i] // whole), surplus)
            holding[i] = holding[i] + addition
            surplus = surplus - addition
    return np.array(holding)


def normal_values(rng, extent, deviation, limit, shards=(), kind=jnp.bfloat16):
    level = levels(rng, extent, shards, -0.22, 0.18) if shards else 1.0
    result = jax.random.normal(rng, extent, jnp.float32) * deviation * level
    return jnp.minimum(jnp.maximum(result, -limit), limit).astype(kind)


def setup_inputs(seed: int = 0, part: int = 0) -> dict:
    keys = jax.random.split(jax.random.key(seed), 17)
    own_keys = jax.random.split(jax.random.fold_in(keys[16], part), 17)
    tokens_in = draw_tokens_in(jax.random.fold_in(jax.random.fold_in(keys[16], part), 71), part)
    norm_gain = jnp.clip(1.0 + 0.18 * jax.random.normal(keys[1], (D,), jnp.float32), 0.1, 1.9)
    w_qkv = normal_values(keys[2], (D, QKVW), D ** -0.5, 0.078125, ((0, 16),))
    w_out = normal_values(keys[3], (D, D), D ** -0.5, 0.078125, ((1, 16),))
    cache_keys = draw_cache_keys(jax.random.fold_in(jax.random.fold_in(keys[16], part), 71), part)
    cache_values = normal_values(own_keys[5], (REQ, CACHE, KVH * HD), 1.0, 6.0, ((0, 16),))
    kv_lengths = draw_kv_lengths(jax.random.fold_in(jax.random.fold_in(keys[16], part), 71), part)
    w_cond = normal_values(keys[7], (D, HW), D ** -0.5, 0.078125, ((0, 16),))
    w_embed = normal_values(keys[8], (LAT, D), LAT ** -0.5, 1.5, ((1, 16),))
    placement_keys = jax.random.split(jax.random.fold_in(own_keys[9], 1), REQ // REQ)
    placement_turns = jax.random.permutation(jax.random.fold_in(own_keys[9], 3), REQ // REQ)
    placement = jax.vmap(lambda own, number: deal_out(jax.random.fold_in(own_keys[9], 2), own, number, REQ, N_TENSOR, 1, HCAP, 2))(placement_keys, placement_turns).reshape((REQ, 1))
    noise = normal_values(own_keys[10], (2, SLOTS, LAT), 1.0, 5.0, ((1, 16),), jnp.float32)
    w_latent = normal_values(keys[11], (LAT, HW), LAT ** -0.5, 1.5)
    w_up = normal_values(keys[12], (HW, HW), HW ** -0.5, 0.15625)
    w_down = normal_values(keys[13], (HW, HW), HW ** -0.5, 0.15625)
    w_vel = normal_values(keys[14], (HW, LAT), HW ** -0.5, 0.15625)
    head_gain = jnp.clip(1.0 + 0.18 * jax.random.normal(keys[15], (HW,), jnp.float32), 0.1, 1.9)
    return {"tokens_in": tokens_in, "norm_gain": norm_gain, "w_qkv": w_qkv, "w_out": w_out, "cache_keys": cache_keys, "cache_values": cache_values, "kv_lengths": kv_lengths, "w_cond": w_cond, "w_embed": w_embed, "placement": placement, "noise": noise, "w_latent": w_latent, "w_up": w_up, "w_down": w_down, "w_vel": w_vel, "head_gain": head_gain}


def slot_numbers(placement, devices):
    owner = placement[:, 0]
    onehot = (owner[:, None] == jnp.arange(devices, dtype=jnp.int32)[None, :]).astype(jnp.int32)
    before = jnp.cumsum(onehot, axis=0) - onehot
    rank = lax.optimization_barrier(jnp.sum(before * onehot, axis=1))
    return (owner * HCAP + rank).astype(jnp.int32)

def time_table(number):
    half = HW // 2
    freqs = jnp.exp(-math.log(10000.0) * jnp.arange(half, dtype=jnp.float32) / half)
    angle = 1000.0 * number / STEPS * freqs
    return jnp.concatenate([jnp.sin(angle), jnp.cos(angle)])

def denoise(latent, condition, w_latent, w_up, w_down, w_vel, head_gain):
    for number in range(STEPS):
        act = jnp.dot(latent.astype(jnp.bfloat16), w_latent, preferred_element_type=jnp.float32)
        act = act + condition.astype(jnp.float32) + time_table(number)[None, :]
        normact = (act * lax.rsqrt(lax.optimization_barrier(jnp.mean(act * act, axis=1, keepdims=True)) + 1e-05) * head_gain).astype(jnp.bfloat16)
        inner = jax.nn.silu(jnp.dot(normact, w_up, preferred_element_type=jnp.float32)).astype(jnp.bfloat16)
        block = act + jnp.dot(inner, w_down, preferred_element_type=jnp.float32)
        normblock = (block * lax.rsqrt(lax.optimization_barrier(jnp.mean(block * block, axis=1, keepdims=True)) + 1e-05)).astype(jnp.bfloat16)
        latent = latent + jnp.dot(normblock, w_vel, preferred_element_type=jnp.float32) / STEPS
    return latent

def attend(query, cache_keys, cache_values, lengths, extra_keys, extra_values):
    rows = query.shape[0]
    cached = cache_keys.shape[1]
    extra = extra_keys.shape[1]
    group = HEADS // KVH
    queries = query.reshape(rows, KVH, group, HD).astype(jnp.float32)
    keys_c = cache_keys.reshape(rows, cached, KVH, HD).astype(jnp.float32)
    vals_c = cache_values.reshape(rows, cached, KVH, HD).astype(jnp.float32)
    keys_e = extra_keys.reshape(rows, extra, KVH, HD).astype(jnp.float32)
    vals_e = extra_values.reshape(rows, extra, KVH, HD).astype(jnp.float32)
    scale = 1.0 / math.sqrt(HD)
    score_c = jnp.einsum('rkgd,rckd->rkgc', queries, keys_c) * scale
    live = jnp.arange(cached, dtype=jnp.int32)[None, :] < lengths[:, None]
    score_c = jnp.where(live[:, None, None, :], score_c, -1e+30)
    score_e = jnp.einsum('rkgd,rekd->rkge', queries, keys_e) * scale
    top = jnp.maximum(lax.optimization_barrier(jnp.max(score_c, axis=3)), lax.optimization_barrier(jnp.max(score_e, axis=3)))
    prob_c = jnp.exp(score_c - top[..., None])
    prob_e = jnp.exp(score_e - top[..., None])
    total = lax.optimization_barrier(jnp.sum(prob_c, axis=3)) + lax.optimization_barrier(jnp.sum(prob_e, axis=3))
    weight_c = (prob_c / total[..., None]).astype(jnp.bfloat16).astype(jnp.float32)
    weight_e = (prob_e / total[..., None]).astype(jnp.bfloat16).astype(jnp.float32)
    mixed = jnp.einsum('rkgc,rckd->rkgd', weight_c, vals_c) + jnp.einsum('rkge,rekd->rkgd', weight_e, vals_e)
    return mixed.reshape(rows, HEADS * HD).astype(jnp.bfloat16)

def reference(tokens_in, norm_gain, w_qkv, w_out, cache_keys, cache_values, kv_lengths, w_cond, w_embed, placement, noise, w_latent, w_up, w_down, w_vel, head_gain):
    slot = slot_numbers(placement, N_TENSOR)
    inputs = tokens_in
    extra_keys = jnp.zeros((REQ, 0, KVH * HD), jnp.bfloat16)
    extra_values = jnp.zeros((REQ, 0, KVH * HD), jnp.bfloat16)
    results = []
    decoded = inputs
    for decode_index in range(2):
        floats = inputs.astype(jnp.float32)
        rms = jnp.sqrt(lax.optimization_barrier(jnp.sum(floats * floats, axis=1)) / D + 1e-06)
        normed = (floats * norm_gain[None, :] / rms[:, None]).astype(jnp.bfloat16)
        qkv = jnp.dot(normed, w_qkv, preferred_element_type=jnp.float32).astype(jnp.bfloat16)
        query = qkv[:, :HEADS * HD]
        new_key = qkv[:, HEADS * HD:(HEADS + KVH) * HD]
        new_value = qkv[:, (HEADS + KVH) * HD:]
        extra_keys = jnp.concatenate([extra_keys, new_key[:, None, :]], axis=1)
        extra_values = jnp.concatenate([extra_values, new_value[:, None, :]], axis=1)
        attended = attend(query, cache_keys, cache_values, kv_lengths, extra_keys, extra_values)
        decoded = (floats + jnp.dot(attended, w_out, preferred_element_type=jnp.float32)).astype(jnp.bfloat16)
        condition = jnp.dot(decoded, w_cond, preferred_element_type=jnp.float32).astype(jnp.bfloat16)
        start = noise[decode_index][slot]
        latent = denoise(start, condition, w_latent, w_up, w_down, w_vel, head_gain)
        results.append(latent)
        inputs = jnp.dot(latent.astype(jnp.bfloat16), w_embed, preferred_element_type=jnp.float32).astype(jnp.bfloat16)
    return (jnp.stack(results), decoded)
```

```python
import functools
import math

import numpy as np

import jax
import jax.numpy as jnp
from jax import lax
from jax.experimental import pallas as pl
from jax.experimental.pallas import tpu as pltpu
from jax.sharding import PartitionSpec as P

D = 5120
HEADS = 40
KVH = 8
HD = 128
GRP = HEADS // KVH
HW = 1536
LAT = 16
STEPS = 8
HCAP = 8
LANE = 128
F32 = jnp.float32
BF16 = jnp.bfloat16

QROWS = 128
AROWS = (80, 96)
CROWS = 32
NPHASE = 8
NOISE, QKV, WSUM, WALL = 0, 1, 2, 3


def time_tables():
    half = HW // 2
    freqs = np.exp(-math.log(10000.0) * np.arange(half, dtype=np.float64) / half)
    angle = 1000.0 * np.arange(STEPS, dtype=np.float64)[:, None] / STEPS * freqs[None, :]
    return np.concatenate([np.sin(angle), np.cos(angle)], axis=1).astype(np.float32)


def column_tile(t, j):
    if t < GRP:
        return GRP * j + t
    return HEADS + (t - GRP) * KVH + j


def dot(a, b):
    return jnp.dot(a, b, preferred_element_type=F32)


def dot_t(a, b):
    return lax.dot_general(a, b, (((1,), (1,)), ((), ())), preferred_element_type=F32)


def kernel(
    n,
    tiles,
    x_ref,
    gain_ref,
    wqkv_hbm,
    wout_hbm,
    ck_hbm,
    cv_hbm,
    kvl_ref,
    wcond_hbm,
    wemb_ref,
    plc_ref,
    noise_ref,
    wlat_ref,
    wup_hbm,
    wdown_hbm,
    wvel_ref,
    hgain_ref,
    table_ref,
    lat_out,
    hid_out,
    wqkv,
    wout,
    ck,
    cv,
    wcond,
    wup,
    wdown,
    qkv32,
    qkv_send,
    qkv_recv,
    w_send,
    w_recv,
    w_all,
    noise_all,
    att0_all,
    att1_all,
    att32,
    gathered,
    cond32,
    cond_send0,
    cond_send1,
    cond_recv0,
    cond_recv1,
    cond_own,
    load_sem,
    send_sem,
    recv_sem,
):
    me = lax.axis_index("tensor")
    rows = x_ref.shape[0]

    loads = [
        pltpu.make_async_copy(src, dst, load_sem.at[k])
        for k, (src, dst) in enumerate(
            [
                (wqkv_hbm, wqkv),
                (ck_hbm, ck),
                (cv_hbm, cv),
                (wout_hbm, wout),
                (wcond_hbm, wcond),
                (wup_hbm, wup),
                (wdown_hbm, wdown),
            ]
        )
    ]
    for load in loads:
        load.start()

    barrier = pltpu.get_barrier_semaphore()

    def greet(k, c):
        peer = lax.rem(me + k, n)
        pl.semaphore_signal(
            barrier, inc=1, device_id={"tensor": peer}, device_id_type=pl.DeviceIdType.MESH
        )
        return c

    lax.fori_loop(1, n, greet, 0)

    def block(ref, index, size):
        return ref.at[pl.ds(pl.multiple_of(index * size, size), size), :]

    def copy(phase, src, dst, peer, origin):
        return pltpu.make_async_remote_copy(
            src_ref=src,
            dst_ref=dst,
            send_sem=send_sem.at[phase, peer],
            recv_sem=recv_sem.at[phase, origin],
            device_id={"tensor": peer},
            device_id_type=pl.DeviceIdType.MESH,
        )

    def gather_start(phase, buf, size):
        def body(k, c):
            peer = lax.rem(me + k, n)
            copy(phase, block(buf, me, size), block(buf, me, size), peer, me).start()
            return c

        lax.fori_loop(1, n, body, 0)

    def gather_wait(phase, buf, size):
        def body(k, c):
            peer = lax.rem(me + n - k, n)
            copy(phase, block(buf, me, size), block(buf, peer, size), peer, peer).wait()
            return c

        lax.fori_loop(1, n, body, 0)

    def scatter_start(phase, wide, send, recv, size):
        def body(k, c):
            peer = lax.rem(me + k, n)
            if wide is not None:
                block(send, peer, size)[...] = block(wide, peer, size)[...].astype(BF16)
            copy(phase, block(send, peer, size), block(recv, me, size), peer, me).start()
            return c

        lax.fori_loop(1, n, body, 0)

    def scatter_sum(phase, own, send, recv, size):
        def body(k, acc):
            peer = lax.rem(me + n - k, n)
            copy(phase, block(send, peer, size), block(recv, peer, size), peer, peer).wait()
            return acc + block(recv, peer, size)[...].astype(F32)

        return lax.fori_loop(1, n, body, own)

    to = lax.broadcasted_iota(jnp.int32, (rows, rows), 0)
    frm = lax.broadcasted_iota(jnp.int32, (rows, rows), 1)
    perm = jnp.where(frm == lax.rem(to, n) * 2 + to // n, 1.0, 0.0).astype(BF16)
    back = jnp.where(to == lax.rem(frm, n) * 2 + frm // n, 1.0, 0.0).astype(BF16)

    x0 = dot(perm, x_ref[...])
    squares = jnp.sum(x0 * x0, axis=1, keepdims=True)
    squares = jnp.broadcast_to(squares, (rows, LANE))
    high = squares.astype(BF16).astype(F32)
    embed = wemb_ref[...]
    gain = gain_ref[...]
    left = jnp.concatenate(
        [(x0 * gain).astype(BF16), (embed.astype(F32) * gain).astype(BF16)], axis=0
    )

    block(noise_all, me, HCAP)[...] = jnp.concatenate(
        [noise_ref[0], noise_ref[1], jnp.zeros((HCAP, LANE - 2 * LAT), F32)], axis=1
    )

    pl.semaphore_wait(barrier, n - 1)
    gather_start(NOISE, noise_all, HCAP)

    def place(value, row):
        for i in range(2):
            qkv32[pl.ds(row + i * 8, n, stride=QROWS), :] = value[i * n : (i + 1) * n, :]

    for j in range(KVH):
        place(high if j == 0 else squares - high, 7 * 16 + j)

    loads[0].wait()
    where_to = {column_tile(t, j): (t, j) for t in range(7) for j in range(KVH)}
    wide = 512
    for c in range(0, wqkv.shape[1], wide):
        part = dot(left, wqkv[:, c : c + wide])
        for s in range(wide // LANE):
            t, j = where_to[c // LANE + s]
            piece = part[:, s * LANE : (s + 1) * LANE]
            place(piece[:rows], t * 16 + j)
            at = (t * KVH + j) * LAT
            w_send[at : at + LAT, :] = piece[rows:].astype(BF16)
    scatter_start(QKV, qkv32, qkv_send, qkv_recv, QROWS)

    gram = dot_t(embed, embed)
    gram = jnp.concatenate([gram, jnp.zeros((LAT, LANE - LAT), F32)], axis=1)
    gram_high = gram.astype(BF16)
    w_send[56 * LAT : 57 * LAT, :] = gram_high
    w_send[57 * LAT : 58 * LAT, :] = (gram - gram_high.astype(F32)).astype(BF16)
    w_send[58 * LAT :, :] = jnp.zeros((w_send.shape[0] - 58 * LAT, LANE), BF16)
    cond32[...] = jnp.zeros(cond32.shape, F32)

    gather_wait(NOISE, noise_all, HCAP)
    owner = plc_ref[...].astype(F32)
    index = lax.broadcasted_iota(jnp.int32, (rows, 1), 0)
    slots = lax.broadcasted_iota(jnp.int32, (n * HCAP, 1), 0).astype(F32)
    picked = []
    for i in range(2):
        row = me * 2 + i
        mine = jnp.sum(jnp.where(index == row, owner, 0.0), axis=0, keepdims=True)
        before = jnp.where((owner == mine) & (index < row), 1.0, 0.0)
        slot = mine * HCAP + jnp.sum(before, axis=0, keepdims=True)
        picked.append(
            jnp.sum(jnp.where(slots == slot, noise_all[...], 0.0), axis=0, keepdims=True)
        )
    picked = jnp.concatenate(picked + [jnp.zeros((6, LANE), F32)], axis=0)

    sums = scatter_sum(QKV, block(qkv32, me, QROWS)[...], qkv_send, qkv_recv, QROWS)
    loads[1].wait()
    loads[2].wait()

    head = lax.broadcasted_iota(jnp.int32, (HEADS, LANE), 0) % KVH
    scale = 1.0 / math.sqrt(HD)

    def per_head(value):
        return jnp.concatenate([value] * GRP, axis=0)

    def attend(i, query, extra):
        spread = jnp.concatenate(
            [jnp.where(head == k, query, 0.0) for k in range(KVH)], axis=1
        ).astype(BF16)
        score = dot_t(spread, ck[i]) * scale
        slot = lax.broadcasted_iota(jnp.int32, score.shape, 1)
        score = jnp.where(slot < kvl_ref[i], score, -1e30)
        own = [jnp.sum(query * per_head(k), axis=1, keepdims=True) * scale for k, _ in extra]
        top = jnp.max(score, axis=1, keepdims=True)
        for s in own:
            top = jnp.maximum(top, s)
        prob = jnp.exp(score - top)
        prob_own = [jnp.exp(s - top) for s in own]
        total = jnp.sum(prob, axis=1, keepdims=True)
        for p in prob_own:
            total = total + p
        full = dot((prob / total).astype(BF16), cv[i])
        mixed = jnp.zeros((HEADS, LANE), F32)
        for k in range(KVH):
            mixed = mixed + jnp.where(head == k, full[:, k * LANE : (k + 1) * LANE], 0.0)
        for p, (_, v) in zip(prob_own, extra):
            mixed = mixed + (p / total).astype(BF16).astype(F32) * per_head(v)
        return mixed

    def rounded(value):
        return value.astype(BF16).astype(F32)

    def split(tile_of, inverse, i):
        part = [rounded(tile_of(t, i) * inverse) for t in range(7)]
        return jnp.concatenate(part[:GRP], axis=0), part[GRP], part[GRP + 1]

    def mixed_rows(outs):
        return jnp.concatenate(
            [outs[i][t * 8 : (t + 1) * 8] for t in range(GRP) for i in range(2)], axis=0
        ).astype(BF16)

    def project(att_all, size, inputs):
        att32[pl.ds(0, n * size), :] = att_all[...].astype(F32)
        for t in range(GRP):
            for j in range(KVH):
                h = GRP * j + t
                both = [
                    att32[pl.ds(t * 16 + i * 8 + j, n, stride=size), :] for i in range(2)
                ]
                gathered[:, h * LANE : (h + 1) * LANE] = jnp.concatenate(both, axis=0).astype(
                    BF16
                )
        if inputs is None:
            both = [att32[pl.ds(80 + i * 8, n, stride=size), :] for i in range(2)]
            tokens = jnp.concatenate(both, axis=0)[:, :LAT].astype(BF16)
            inputs = rounded(dot(tokens, embed))
        return (inputs + dot(gathered[...], wout[...])).astype(BF16)

    def send_condition(phase, decoded, send, recv):
        cond = dot(decoded, wcond[...])
        for u in range(HW // LANE):
            for i in range(2):
                cond32[pl.ds(u * 2 + i, n, stride=CROWS), :] = cond[
                    i * n : (i + 1) * n, u * LANE : (u + 1) * LANE
                ]
        scatter_start(phase, cond32, send, recv, CROWS)

    def take_condition(phase, send, recv):
        total = scatter_sum(phase, block(cond32, me, CROWS)[...], send, recv, CROWS)
        total = rounded(total)
        cond_own[...] = jnp.zeros(cond_own.shape, F32)
        for u in range(HW // LANE):
            cond_own[0:2, u * LANE : (u + 1) * LANE] = total[2 * u : 2 * u + 2, :]

    def denoise(first, last, latent):
        def body(k, latent):
            act = dot(latent.astype(BF16), wlat_ref[...])
            act = act + cond_own[...] + table_ref[pl.ds(k, 1), :]
            inv = lax.rsqrt(jnp.mean(act * act, axis=1, keepdims=True) + 1e-05)
            norm = (act * inv * hgain_ref[...]).astype(BF16)
            inner = jax.nn.silu(dot(norm, wup[...])).astype(BF16)
            out = act + dot(inner, wdown[...])
            inv = lax.rsqrt(jnp.mean(out * out, axis=1, keepdims=True) + 1e-05)
            return latent + dot((out * inv).astype(BF16), wvel_ref[...]) / STEPS

        return lax.fori_loop(first, last, body, latent)

    outs, kept = [], []
    for i in range(2):
        base = 7 * 16 + i * 8
        square = sums[base : base + 1, 0:1] + sums[base + 1 : base + 2, 0:1]
        inverse = 1.0 / jnp.sqrt(square / D + 1e-06)
        query, key, value = split(
            lambda t, i: sums[t * 16 + i * 8 : t * 16 + i * 8 + 8], inverse, i
        )
        kept.append((key, value))
        outs.append(attend(i, query, [(key, value)]))
    block(att0_all, me, AROWS[0])[...] = mixed_rows(outs)
    gather_start(4, att0_all, AROWS[0])
    loads[3].wait()
    loads[4].wait()
    gather_wait(4, att0_all, AROWS[0])
    decoded = project(att0_all, AROWS[0], x0)
    send_condition(5, decoded, cond_send0, cond_recv0)
    scatter_start(WSUM, None, w_send, w_recv, tiles * LAT)
    loads[5].wait()
    loads[6].wait()
    take_condition(5, cond_send0, cond_recv0)
    latent = denoise(0, STEPS // 2, picked[:, :LAT])
    size = tiles * LAT
    total = scatter_sum(WSUM, block(w_send, me, size)[...].astype(F32), w_send, w_recv, size)
    block(w_all, me, size)[...] = total.astype(BF16)
    gather_start(WALL, w_all, size)
    latent = denoise(STEPS // 2, STEPS, latent)
    lat_out[0] = latent[0:2]
    gather_wait(WALL, w_all, size)

    token = latent.astype(BF16)
    form = dot(token, w_all[56 * LAT : 57 * LAT, :]) + dot(token, w_all[57 * LAT : 58 * LAT, :])
    square = jnp.sum(form[:, :LAT] * token.astype(F32), axis=1, keepdims=True)
    inverse = 1.0 / jnp.sqrt(jnp.maximum(square, 0.0) / D + 1e-06)
    token = token.astype(F32)
    lane = lax.broadcasted_iota(jnp.int32, (KVH, LANE), 1) // LAT
    which = lax.broadcasted_iota(jnp.int32, (KVH, LANE), 0)
    spread = []
    for i in range(2):
        eight = jnp.concatenate([token[i : i + 1, :]] * KVH, axis=1)
        spread.append(jnp.where(lane == which, jnp.broadcast_to(eight, (KVH, LANE)), 0.0))
    spread = jnp.concatenate(spread, axis=0).astype(BF16)
    second = [dot(spread, w_all[t * LANE : (t + 1) * LANE, :]) for t in range(7)]
    outs = []
    for i in range(2):
        query, key, value = split(
            lambda t, i: second[t][i * 8 : i * 8 + 8], inverse[i : i + 1], i
        )
        outs.append(attend(i, query, [kept[i], (key, value)]))
    sent = jnp.concatenate(
        [token, jnp.zeros((8, LANE - LAT), F32)], axis=1
    )
    sent = [jnp.broadcast_to(sent[i : i + 1, :], (8, LANE)) for i in range(2)]
    block(att1_all, me, AROWS[1])[...] = jnp.concatenate(
        [mixed_rows(outs), jnp.concatenate(sent, axis=0).astype(BF16)], axis=0
    )
    gather_start(6, att1_all, AROWS[1])
    gather_wait(6, att1_all, AROWS[1])
    decoded = project(att1_all, AROWS[1], None)
    send_condition(7, decoded, cond_send1, cond_recv1)
    hid_out[...] = dot(back, decoded).astype(BF16)
    take_condition(7, cond_send1, cond_recv1)
    latent = denoise(0, STEPS, picked[:, LAT : 2 * LAT])
    lat_out[1] = latent[0:2]


def per_device(
    tokens_in,
    norm_gain,
    w_qkv,
    w_out,
    cache_keys,
    cache_values,
    kv_lengths,
    w_cond,
    w_embed,
    placement,
    noise,
    w_latent,
    w_up,
    w_down,
    w_vel,
    head_gain,
):
    n = lax.axis_size("tensor")
    rows, own = tokens_in.shape
    tiles = -(-64 // n)
    total = tiles * n
    vmem = pl.BlockSpec(memory_space=pltpu.VMEM)
    smem = pl.BlockSpec(memory_space=pltpu.SMEM)
    hbm = pl.BlockSpec(memory_space=pl.ANY)
    scratch = [
        pltpu.VMEM(w_qkv.shape, BF16),
        pltpu.VMEM(w_out.shape, BF16),
        pltpu.VMEM(cache_keys.shape, BF16),
        pltpu.VMEM(cache_values.shape, BF16),
        pltpu.VMEM(w_cond.shape, BF16),
        pltpu.VMEM(w_up.shape, BF16),
        pltpu.VMEM(w_down.shape, BF16),
        pltpu.VMEM((n * QROWS, LANE), F32),
        pltpu.VMEM((n * QROWS, LANE), BF16),
        pltpu.VMEM((n * QROWS, LANE), BF16),
        pltpu.VMEM((total * LAT, LANE), BF16),
        pltpu.VMEM((total * LAT, LANE), BF16),
        pltpu.VMEM((total * LAT, LANE), BF16),
        pltpu.VMEM((n * HCAP, LANE), F32),
        pltpu.VMEM((n * AROWS[0], LANE), BF16),
        pltpu.VMEM((n * AROWS[1], LANE), BF16),
        pltpu.VMEM((n * AROWS[1], LANE), F32),
        pltpu.VMEM((rows, D), BF16),
        pltpu.VMEM((n * CROWS, LANE), F32),
        pltpu.VMEM((n * CROWS, LANE), BF16),
        pltpu.VMEM((n * CROWS, LANE), BF16),
        pltpu.VMEM((n * CROWS, LANE), BF16),
        pltpu.VMEM((n * CROWS, LANE), BF16),
        pltpu.VMEM((8, HW), F32),
        pltpu.SemaphoreType.DMA((7,)),
        pltpu.SemaphoreType.DMA((NPHASE, n)),
        pltpu.SemaphoreType.DMA((NPHASE, n)),
    ]
    return pl.pallas_call(
        functools.partial(kernel, n, tiles),
        out_shape=(
            jax.ShapeDtypeStruct((2, rows // n, LAT), F32),
            jax.ShapeDtypeStruct((rows, own), BF16),
        ),
        in_specs=[
            vmem, vmem, hbm, hbm, hbm, hbm, smem, hbm, vmem, vmem, vmem, vmem, hbm, hbm, vmem,
            vmem, vmem,
        ],
        out_specs=(vmem, vmem),
        scratch_shapes=scratch,
        compiler_params=pltpu.CompilerParams(
            collective_id=0, has_side_effects=True, vmem_limit_bytes=50 * 1024 * 1024
        ),
    )(
        tokens_in,
        norm_gain[None, :],
        w_qkv,
        w_out,
        cache_keys,
        cache_values,
        kv_lengths,
        w_cond,
        w_embed,
        placement,
        noise,
        w_latent,
        w_up,
        w_down,
        w_vel,
        head_gain[None, :],
        jnp.asarray(time_tables()),
    )


def solution(mesh):
    return jax.shard_map(
        per_device,
        mesh=mesh,
        in_specs=(
            P("group", "tensor"),
            P("tensor"),
            P("tensor", None),
            P(None, "tensor"),
            P(("group", "tensor"), None, None),
            P(("group", "tensor"), None, None),
            P(("group", "tensor")),
            P("tensor", None),
            P(None, "tensor"),
            P("group", None),
            P(None, ("group", "tensor"), None),
            P(),
            P(),
            P(),
            P(),
            P(),
        ),
        out_specs=(P(None, ("group", "tensor"), None), P("group", "tensor")),
        check_vma=False,
    )
```

```python
import functools
import math

import numpy as np

import jax
import jax.numpy as jnp
from jax import lax
from jax.experimental import pallas as pl
from jax.experimental.pallas import tpu as pltpu
from jax.sharding import PartitionSpec as P

D = 5120
HEADS = 40
KVH = 8
HD = 128
GRP = HEADS // KVH
HW = 1536
LAT = 16
STEPS = 8
HCAP = 8
LANE = 128
F32 = jnp.float32
BF16 = jnp.bfloat16

QROWS = 128
AROWS = (80, 96)
CROWS = 32
NPHASE = 8
NOISE, QKV, WSUM, WALL = 0, 1, 2, 3


def time_tables():
    half = HW // 2
    freqs = np.exp(-math.log(10000.0) * np.arange(half, dtype=np.float64) / half)
    angle = 1000.0 * np.arange(STEPS, dtype=np.float64)[:, None] / STEPS * freqs[None, :]
    return np.concatenate([np.sin(angle), np.cos(angle)], axis=1).astype(np.float32)


def column_tile(t, j):
    if t < GRP:
        return GRP * j + t
    return HEADS + (t - GRP) * KVH + j


def dot(a, b):
    return jnp.dot(a, b, preferred_element_type=F32)


def dot_t(a, b):
    return lax.dot_general(a, b, (((1,), (1,)), ((), ())), preferred_element_type=F32)


def kernel(
    n,
    tiles,
    x_ref,
    gain_ref,
    wqkv_hbm,
    wout_hbm,
    ck_hbm,
    cv_hbm,
    kvl_ref,
    wcond_hbm,
    wemb_ref,
    plc_ref,
    noise_ref,
    wlat_ref,
    wup_hbm,
    wdown_hbm,
    wvel_ref,
    hgain_ref,
    table_ref,
    lat_out,
    hid_out,
    wqkv,
    wout,
    ck,
    cv,
    wcond,
    wup,
    wdown,
    qkv32,
    qkv_send,
    qkv_recv,
    w_send,
    w_recv,
    w_all,
    noise_all,
    att0_all,
    att1_all,
    att32,
    gathered,
    cond32,
    cond_send0,
    cond_send1,
    cond_recv0,
    cond_recv1,
    cond_own,
    load_sem,
    send_sem,
    recv_sem,
):
    me = lax.axis_index("tensor")
    rows = x_ref.shape[0]

    loads = [
        pltpu.make_async_copy(src, dst, load_sem.at[k])
        for k, (src, dst) in enumerate(
            [
                (wqkv_hbm, wqkv),
                (ck_hbm, ck),
                (cv_hbm, cv),
                (wout_hbm, wout),
                (wcond_hbm, wcond),
                (wup_hbm, wup),
                (wdown_hbm, wdown),
            ]
        )
    ]
    for load in loads:
        load.start()

    barrier = pltpu.get_barrier_semaphore()

    def greet(k, c):
        peer = lax.rem(me + k, n)
        pl.semaphore_signal(
            barrier, inc=1, device_id={"tensor": peer}, device_id_type=pl.DeviceIdType.MESH
        )
        return c

    lax.fori_loop(1, n, greet, 0)

    def block(ref, index, size):
        return ref.at[pl.ds(pl.multiple_of(index * size, size), size), :]

    def copy(phase, src, dst, peer, origin):
        return pltpu.make_async_remote_copy(
            src_ref=src,
            dst_ref=dst,
            send_sem=send_sem.at[phase, peer],
            recv_sem=recv_sem.at[phase, origin],
            device_id={"tensor": peer},
            device_id_type=pl.DeviceIdType.MESH,
        )

    def gather_start(phase, buf, size):
        def body(k, c):
            peer = lax.rem(me + k, n)
            copy(phase, block(buf, me, size), block(buf, me, size), peer, me).start()
            return c

        lax.fori_loop(1, n, body, 0)

    def gather_wait(phase, buf, size):
        def body(k, c):
            peer = lax.rem(me + n - k, n)
            copy(phase, block(buf, me, size), block(buf, peer, size), peer, peer).wait()
            return c

        lax.fori_loop(1, n, body, 0)

    def scatter_start(phase, wide, send, recv, size):
        def body(k, c):
            peer = lax.rem(me + k, n)
            if wide is not None:
                block(send, peer, size)[...] = block(wide, peer, size)[...].astype(BF16)
            copy(phase, block(send, peer, size), block(recv, me, size), peer, me).start()
            return c

        lax.fori_loop(1, n, body, 0)

    def scatter_sum(phase, own, send, recv, size):
        def body(k, acc):
            peer = lax.rem(me + n - k, n)
            copy(phase, block(send, peer, size), block(recv, peer, size), peer, peer).wait()
            return acc + block(recv, peer, size)[...].astype(F32)

        return lax.fori_loop(1, n, body, own)

    to = lax.broadcasted_iota(jnp.int32, (rows, rows), 0)
    frm = lax.broadcasted_iota(jnp.int32, (rows, rows), 1)
    perm = jnp.where(frm == lax.rem(to, n) * 2 + to // n, 1.0, 0.0).astype(BF16)
    back = jnp.where(to == lax.rem(frm, n) * 2 + frm // n, 1.0, 0.0).astype(BF16)

    x0 = dot(perm, x_ref[...])
    squares = jnp.sum(x0 * x0, axis=1, keepdims=True)
    squares = jnp.broadcast_to(squares, (rows, LANE))
    high = squares.astype(BF16).astype(F32)
    embed = wemb_ref[...]
    gain = gain_ref[...][None, :]
    head_gain = hgain_ref[...][None, :]
    left = jnp.concatenate(
        [(x0 * gain).astype(BF16), (embed.astype(F32) * gain).astype(BF16)], axis=0
    )

    block(noise_all, me, HCAP)[...] = jnp.concatenate(
        [noise_ref[0], noise_ref[1], jnp.zeros((HCAP, LANE - 2 * LAT), F32)], axis=1
    )

    pl.semaphore_wait(barrier, n - 1)
    gather_start(NOISE, noise_all, HCAP)

    def place(value, row):
        for i in range(2):
            qkv32[pl.ds(row + i * 8, n, stride=QROWS), :] = value[i * n : (i + 1) * n, :]

    for j in range(KVH):
        place(high if j == 0 else squares - high, 7 * 16 + j)

    loads[0].wait()
    where_to = {column_tile(t, j): (t, j) for t in range(7) for j in range(KVH)}
    wide = 512
    for c in range(0, wqkv.shape[1], wide):
        part = dot(left, wqkv[:, c : c + wide])
        for s in range(wide // LANE):
            t, j = where_to[c // LANE + s]
            piece = part[:, s * LANE : (s + 1) * LANE]
            place(piece[:rows], t * 16 + j)
            at = (t * KVH + j) * LAT
            w_send[at : at + LAT, :] = piece[rows:].astype(BF16)
    scatter_start(QKV, qkv32, qkv_send, qkv_recv, QROWS)

    gram = dot_t(embed, embed)
    gram = jnp.concatenate([gram, jnp.zeros((LAT, LANE - LAT), F32)], axis=1)
    gram_high = gram.astype(BF16)
    w_send[56 * LAT : 57 * LAT, :] = gram_high
    w_send[57 * LAT : 58 * LAT, :] = (gram - gram_high.astype(F32)).astype(BF16)
    w_send[58 * LAT :, :] = jnp.zeros((w_send.shape[0] - 58 * LAT, LANE), BF16)
    cond32[...] = jnp.zeros(cond32.shape, F32)

    gather_wait(NOISE, noise_all, HCAP)
    owner = plc_ref[...].astype(F32)
    index = lax.broadcasted_iota(jnp.int32, (1, rows), 1)
    slots = lax.broadcasted_iota(jnp.int32, (n * HCAP, 1), 0).astype(F32)
    picked = []
    for i in range(2):
        row = me * 2 + i
        mine = jnp.sum(jnp.where(index == row, owner, 0.0), axis=1, keepdims=True)
        before = jnp.where((owner == mine) & (index < row), 1.0, 0.0)
        slot = mine * HCAP + jnp.sum(before, axis=1, keepdims=True)
        picked.append(
            jnp.sum(jnp.where(slots == slot, noise_all[...], 0.0), axis=0, keepdims=True)
        )
    picked = jnp.concatenate(picked + [jnp.zeros((6, LANE), F32)], axis=0)

    sums = scatter_sum(QKV, block(qkv32, me, QROWS)[...], qkv_send, qkv_recv, QROWS)
    loads[1].wait()
    loads[2].wait()

    head = lax.broadcasted_iota(jnp.int32, (HEADS, LANE), 0) % KVH
    scale = 1.0 / math.sqrt(HD)

    def per_head(value):
        return jnp.concatenate([value] * GRP, axis=0)

    def attend(i, query, extra):
        spread = jnp.concatenate(
            [jnp.where(head == k, query, 0.0) for k in range(KVH)], axis=1
        ).astype(BF16)
        score = dot_t(spread, ck[i]) * scale
        slot = lax.broadcasted_iota(jnp.int32, score.shape, 1)
        score = jnp.where(slot < kvl_ref[i], score, -1e30)
        own = [jnp.sum(query * per_head(k), axis=1, keepdims=True) * scale for k, _ in extra]
        top = jnp.max(score, axis=1, keepdims=True)
        for s in own:
            top = jnp.maximum(top, s)
        prob = jnp.exp(score - top)
        prob_own = [jnp.exp(s - top) for s in own]
        total = jnp.sum(prob, axis=1, keepdims=True)
        for p in prob_own:
            total = total + p
        full = dot((prob / total).astype(BF16), cv[i])
        mixed = jnp.zeros((HEADS, LANE), F32)
        for k in range(KVH):
            mixed = mixed + jnp.where(head == k, full[:, k * LANE : (k + 1) * LANE], 0.0)
        for p, (_, v) in zip(prob_own, extra):
            mixed = mixed + (p / total).astype(BF16).astype(F32) * per_head(v)
        return mixed

    def rounded(value):
        return value.astype(BF16).astype(F32)

    def split(tile_of, inverse, i):
        part = [rounded(tile_of(t, i) * inverse) for t in range(7)]
        return jnp.concatenate(part[:GRP], axis=0), part[GRP], part[GRP + 1]

    def mixed_rows(outs):
        return jnp.concatenate(
            [outs[i][t * 8 : (t + 1) * 8] for t in range(GRP) for i in range(2)], axis=0
        ).astype(BF16)

    def project(att_all, size, inputs):
        att32[pl.ds(0, n * size), :] = att_all[...].astype(F32)
        for t in range(GRP):
            for j in range(KVH):
                h = GRP * j + t
                both = [
                    att32[pl.ds(t * 16 + i * 8 + j, n, stride=size), :] for i in range(2)
                ]
                gathered[:, h * LANE : (h + 1) * LANE] = jnp.concatenate(both, axis=0).astype(
                    BF16
                )
        if inputs is None:
            both = [att32[pl.ds(80 + i * 8, n, stride=size), :] for i in range(2)]
            tokens = jnp.concatenate(both, axis=0)[:, :LAT].astype(BF16)
            inputs = rounded(dot(tokens, embed))
        return (inputs + dot_t(gathered[...], wout[...])).astype(BF16)

    def send_condition(phase, decoded, send, recv):
        cond = dot(decoded, wcond[...])
        for u in range(HW // LANE):
            for i in range(2):
                cond32[pl.ds(u * 2 + i, n, stride=CROWS), :] = cond[
                    i * n : (i + 1) * n, u * LANE : (u + 1) * LANE
                ]
        scatter_start(phase, cond32, send, recv, CROWS)

    def take_condition(phase, send, recv):
        total = scatter_sum(phase, block(cond32, me, CROWS)[...], send, recv, CROWS)
        total = rounded(total)
        cond_own[...] = jnp.zeros(cond_own.shape, F32)
        for u in range(HW // LANE):
            cond_own[0:2, u * LANE : (u + 1) * LANE] = total[2 * u : 2 * u + 2, :]

    def denoise(first, last, latent):
        def body(k, latent):
            act = dot(latent.astype(BF16), wlat_ref[...])
            act = act + cond_own[...] + table_ref[pl.ds(k, 1), :]
            inv = lax.rsqrt(jnp.mean(act * act, axis=1, keepdims=True) + 1e-05)
            norm = (act * inv * head_gain).astype(BF16)
            inner = jax.nn.silu(dot(norm, wup[...])).astype(BF16)
            out = act + dot(inner, wdown[...])
            inv = lax.rsqrt(jnp.mean(out * out, axis=1, keepdims=True) + 1e-05)
            return latent + dot_t((out * inv).astype(BF16), wvel_ref[...]) / STEPS

        return lax.fori_loop(first, last, body, latent)

    outs, kept = [], []
    for i in range(2):
        base = 7 * 16 + i * 8
        square = sums[base : base + 1, 0:1] + sums[base + 1 : base + 2, 0:1]
        inverse = 1.0 / jnp.sqrt(square / D + 1e-06)
        query, key, value = split(
            lambda t, i: sums[t * 16 + i * 8 : t * 16 + i * 8 + 8], inverse, i
        )
        kept.append((key, value))
        outs.append(attend(i, query, [(key, value)]))
    block(att0_all, me, AROWS[0])[...] = mixed_rows(outs)
    gather_start(4, att0_all, AROWS[0])
    loads[3].wait()
    loads[4].wait()
    gather_wait(4, att0_all, AROWS[0])
    decoded = project(att0_all, AROWS[0], x0)
    send_condition(5, decoded, cond_send0, cond_recv0)
    scatter_start(WSUM, None, w_send, w_recv, tiles * LAT)
    loads[5].wait()
    loads[6].wait()
    take_condition(5, cond_send0, cond_recv0)
    latent = denoise(0, STEPS // 2, picked[:, :LAT])
    size = tiles * LAT
    total = scatter_sum(WSUM, block(w_send, me, size)[...].astype(F32), w_send, w_recv, size)
    block(w_all, me, size)[...] = total.astype(BF16)
    gather_start(WALL, w_all, size)
    latent = denoise(STEPS // 2, STEPS, latent)
    lat_out[0] = latent[0:2]
    gather_wait(WALL, w_all, size)

    token = latent.astype(BF16)
    form = dot(token, w_all[56 * LAT : 57 * LAT, :]) + dot(token, w_all[57 * LAT : 58 * LAT, :])
    square = jnp.sum(form[:, :LAT] * token.astype(F32), axis=1, keepdims=True)
    inverse = 1.0 / jnp.sqrt(jnp.maximum(square, 0.0) / D + 1e-06)
    token = token.astype(F32)
    lane = lax.broadcasted_iota(jnp.int32, (KVH, LANE), 1) // LAT
    which = lax.broadcasted_iota(jnp.int32, (KVH, LANE), 0)
    spread = []
    for i in range(2):
        eight = jnp.concatenate([token[i : i + 1, :]] * KVH, axis=1)
        spread.append(jnp.where(lane == which, jnp.broadcast_to(eight, (KVH, LANE)), 0.0))
    spread = jnp.concatenate(spread, axis=0).astype(BF16)
    second = [dot(spread, w_all[t * LANE : (t + 1) * LANE, :]) for t in range(7)]
    outs = []
    for i in range(2):
        query, key, value = split(
            lambda t, i: second[t][i * 8 : i * 8 + 8], inverse[i : i + 1], i
        )
        outs.append(attend(i, query, [kept[i], (key, value)]))
    sent = jnp.concatenate(
        [token, jnp.zeros((8, LANE - LAT), F32)], axis=1
    )
    sent = [jnp.broadcast_to(sent[i : i + 1, :], (8, LANE)) for i in range(2)]
    block(att1_all, me, AROWS[1])[...] = jnp.concatenate(
        [mixed_rows(outs), jnp.concatenate(sent, axis=0).astype(BF16)], axis=0
    )
    gather_start(6, att1_all, AROWS[1])
    gather_wait(6, att1_all, AROWS[1])
    decoded = project(att1_all, AROWS[1], None)
    send_condition(7, decoded, cond_send1, cond_recv1)
    hid_out[...] = dot(back, decoded).astype(BF16)
    take_condition(7, cond_send1, cond_recv1)
    latent = denoise(0, STEPS, picked[:, LAT : 2 * LAT])
    lat_out[1] = latent[0:2]


def per_device(
    tokens_in,
    norm_gain,
    w_qkv,
    w_out,
    cache_keys,
    cache_values,
    kv_lengths,
    w_cond,
    w_embed,
    placement,
    noise,
    w_latent,
    w_up,
    w_down,
    w_vel,
    head_gain,
):
    n = lax.axis_size("tensor")
    rows, own = tokens_in.shape
    tiles = -(-64 // n)
    total = tiles * n
    vmem = pl.BlockSpec(memory_space=pltpu.VMEM)
    smem = pl.BlockSpec(memory_space=pltpu.SMEM)
    hbm = pl.BlockSpec(memory_space=pl.ANY)
    scratch = [
        pltpu.VMEM(w_qkv.shape, BF16),
        pltpu.VMEM(w_out.shape[::-1], BF16),
        pltpu.VMEM(cache_keys.shape, BF16),
        pltpu.VMEM(cache_values.shape, BF16),
        pltpu.VMEM(w_cond.shape, BF16),
        pltpu.VMEM(w_up.shape, BF16),
        pltpu.VMEM(w_down.shape, BF16),
        pltpu.VMEM((n * QROWS, LANE), F32),
        pltpu.VMEM((n * QROWS, LANE), BF16),
        pltpu.VMEM((n * QROWS, LANE), BF16),
        pltpu.VMEM((total * LAT, LANE), BF16),
        pltpu.VMEM((total * LAT, LANE), BF16),
        pltpu.VMEM((total * LAT, LANE), BF16),
        pltpu.VMEM((n * HCAP, LANE), F32),
        pltpu.VMEM((n * AROWS[0], LANE), BF16),
        pltpu.VMEM((n * AROWS[1], LANE), BF16),
        pltpu.VMEM((n * AROWS[1], LANE), F32),
        pltpu.VMEM((rows, D), BF16),
        pltpu.VMEM((n * CROWS, LANE), F32),
        pltpu.VMEM((n * CROWS, LANE), BF16),
        pltpu.VMEM((n * CROWS, LANE), BF16),
        pltpu.VMEM((n * CROWS, LANE), BF16),
        pltpu.VMEM((n * CROWS, LANE), BF16),
        pltpu.VMEM((8, HW), F32),
        pltpu.SemaphoreType.DMA((7,)),
        pltpu.SemaphoreType.DMA((NPHASE, n)),
        pltpu.SemaphoreType.DMA((NPHASE, n)),
    ]
    return pl.pallas_call(
        functools.partial(kernel, n, tiles),
        out_shape=(
            jax.ShapeDtypeStruct((2, rows // n, LAT), F32),
            jax.ShapeDtypeStruct((rows, own), BF16),
        ),
        in_specs=[
            vmem, vmem, hbm, hbm, hbm, hbm, smem, hbm, vmem, vmem, vmem, vmem, hbm, hbm, vmem,
            vmem, vmem,
        ],
        out_specs=(vmem, vmem),
        scratch_shapes=scratch,
        compiler_params=pltpu.CompilerParams(
            collective_id=0, has_side_effects=True, vmem_limit_bytes=60 * 1024 * 1024
        ),
    )(
        tokens_in,
        norm_gain,
        w_qkv,
        w_out.T,
        cache_keys,
        cache_values,
        kv_lengths,
        w_cond,
        w_embed,
        placement.T,
        noise,
        w_latent,
        w_up,
        w_down,
        w_vel.T,
        head_gain,
        jnp.asarray(time_tables()),
    )


def solution(mesh):
    return jax.shard_map(
        per_device,
        mesh=mesh,
        in_specs=(
            P("group", "tensor"),
            P("tensor"),
            P("tensor", None),
            P(None, "tensor"),
            P(("group", "tensor"), None, None),
            P(("group", "tensor"), None, None),
            P(("group", "tensor")),
            P("tensor", None),
            P(None, "tensor"),
            P("group", None),
            P(None, ("group", "tensor"), None),
            P(),
            P(),
            P(),
            P(),
            P(),
        ),
        out_specs=(P(None, ("group", "tensor"), None), P("group", "tensor")),
        check_vma=False,
    )
```
